256 devices in a mesh: dp: 16 (over x, y), space: 16 (over z, core).
Axes of the slice: x: 4, y: 4, z: 8, core: 2. Of those that a mesh axis runs over, the one named last changes fastest.
Arguments:
- volume: bfloat16 [16, 32, 32, 32, 128], P('dp', 'space'), may hold values from -6 to 6
- weight: bfloat16 [27, 128, 256], replicated, may hold values from -0.109375 to 0.109375
- cotangent: bfloat16 [16, 32, 32, 32, 256], P('dp', 'space'), may hold values from -6 to 6
Outputs:
- activation: bfloat16 [16, 32, 32, 32, 256], P('dp', 'space')
- input_grad: bfloat16 [16, 32, 32, 32, 128], P('dp', 'space')
- weight_grad: float32 [256, 3456], P(('dp', 'space'))
The draws below stay inside these ranges and needn't reach their ends.
All inputs are finite; a program needn't handle non-finite values.
Results may differ from the reference program's by a relative error of at most 0.0075.
Values may be sent and summed in bfloat16 or wider, within the bound.
No kernel may reach another device: no remote copies, remote signals or barrier semaphores. Data moves between devices by JAX's collectives and lax.ppermute only.
A program may use at most 128 MiB of HBM per device.

```python
import jax
import jax.numpy as jnp
from jax import lax

CIN = 128
COUT = 256
HW = 32
BATCH = 16
DEPTH = 32


def with_spikes(result, own_key, source, target, blocks, factor):
    def block_of(position):
        return (jnp.arange(result.shape[position]) // (result.shape[position] // blocks)).reshape((-1,) + (1,) * (result.ndim - 1 - position))

    near = jax.random.permutation(own_key, blocks)[block_of(target)]
    second = (block_of(target) + blocks // 2) % blocks
    return jnp.where((block_of(source) == near) | (block_of(source) == second), factor * result, result)


def shard_levels(rng, shape, split, low, high):
    def one(axis_at, shards_of):
        steps = jax.random.uniform(jax.random.fold_in(jax.random.fold_in(rng, 6), axis_at), (shards_of,), jnp.float32, low / len(split), high / len(split))
        return jnp.repeat(jnp.exp(steps), shape[axis_at] // shards_of).reshape((-1,) + (1,) * (len(shape) - axis_at - 1))

    loudness = one(*split[0])
    for cut in split[1:]:
        loudness = loudness * one(*cut)
    return loudness


def gaussian(own_key, extent, deviation, bound, cuts=(), kind=jnp.bfloat16):
    array = jax.random.normal(own_key, extent, jnp.float32) * deviation
    if len(cuts) > 0:
        array = shard_levels(own_key, extent, cuts, -0.22, 0.18) * array
    return jnp.clip(array, min=-bound, max=bound).astype(kind)


def bell_draw_with(key, extent, spread, limit, split, heavy, held_as=jnp.bfloat16):
    drawn = spread * jax.random.normal(key, extent, jnp.float32)
    if split:
        drawn = drawn * shard_levels(key, extent, split, -0.22, 0.18)
    return jnp.clip(with_spikes(drawn, jax.random.fold_in(key, 3), *heavy), -limit, limit).astype(held_as)


def setup_inputs(seed: int = 0) -> dict:
    key_of = jax.random.split(jax.random.key(seed), 4)
    volume = gaussian(key_of[0], (BATCH, DEPTH, HW, HW, CIN), 1.0, 6.0, ((0, 16), (1, 16)))
    weight = gaussian(key_of[1], (27, CIN, COUT), (27 * CIN) ** -0.5, 0.109375)
    cotangent = bell_draw_with(key_of[2], (BATCH, DEPTH, HW, HW, COUT), 1.0, 6.0, ((0, 16), (1, 16)), (1, 4, 16, 2.0))
    return {"volume": volume, "weight": weight, "cotangent": cotangent}


def reference(volume, weight, cotangent):
    pad_spec = ((0, 0), (1, 1), (1, 1), (1, 1), (0, 0))
    padded = jnp.pad(volume, pad_spec)
    cot_padded = jnp.pad(cotangent, pad_spec)
    weight_full = weight.astype(jnp.float32)
    rows = DEPTH * HW * HW

    def per_sample(carry, item):
        source, grads = item
        pre = jnp.zeros((rows, COUT), jnp.float32)
        back = jnp.zeros((rows, CIN), jnp.float32)
        flat_grads = grads[1:-1, 1:-1, 1:-1].reshape(rows, COUT).astype(jnp.float32)
        pieces = []
        for k in range(27):
            kd, kh, kw = (k // 9, k // 3 % 3, k % 3)
            taken = source[kd:kd + DEPTH, kh:kh + HW, kw:kw + HW].reshape(rows, CIN).astype(jnp.float32)
            pre = pre + jnp.dot(taken, weight_full[k], precision=lax.Precision.HIGHEST)
            shifted = grads[2 - kd:2 - kd + DEPTH, 2 - kh:2 - kh + HW, 2 - kw:2 - kw + HW].reshape(rows, COUT).astype(jnp.float32)
            back = back + jnp.dot(shifted, weight_full[k].T, precision=lax.Precision.HIGHEST)
            pieces.append(jnp.dot(flat_grads.T, taken, precision=lax.Precision.HIGHEST))
        out = jnp.where(pre >= 0, pre, 0.3 * pre).astype(jnp.bfloat16).reshape(DEPTH, HW, HW, COUT)
        back = back.astype(jnp.bfloat16).reshape(DEPTH, HW, HW, CIN)
        return (carry + jnp.concatenate(pieces, axis=1), (out, back))
    start = jnp.zeros((COUT, 27 * CIN), jnp.float32)
    total, (activation, input_grad) = lax.scan(per_sample, start, (padded, cot_padded))
    weight_grad = total / jnp.sqrt(jnp.float32(BATCH * DEPTH * HW * HW))
    return (activation, input_grad, weight_grad)
```

```python
import jax
import jax.numpy as jnp
from jax import lax
from jax.experimental import pallas as pl
from jax.experimental.pallas import tpu as pltpu
from jax.sharding import PartitionSpec as P

bf16, f32 = jnp.bfloat16, jnp.float32
SIDE = 32
CELLS = SIDE * SIDE
CIN, COUT, TAPS = 128, 256, 27
SLAB = 2
PADDED = CELLS + 2 * SIDE
ROWS = 256
VMEM_LIMIT = 48 << 20
FLOPS = 2 * SLAB * CELLS * TAPS * CIN * COUT


def in_vmem():
    return pl.BlockSpec(memory_space=pltpu.VMEM)


def call(kernel, name, outs, scratch, args):
    single = not isinstance(outs, tuple)
    return pl.pallas_call(
        kernel,
        out_shape=outs,
        in_specs=[in_vmem()] * len(args),
        out_specs=in_vmem() if single else tuple(in_vmem() for _ in outs),
        scratch_shapes=scratch,
        compiler_params=pltpu.CompilerParams(vmem_limit_bytes=VMEM_LIMIT),
        cost_estimate=pl.CostEstimate(flops=FLOPS, bytes_accessed=5 << 20, transcendentals=0),
        name=name,
    )(*args)


def product(a, b):
    return jnp.dot(a, b, preferred_element_type=f32)


def fill_taps(planes, wide, taps):
    col = lax.broadcasted_iota(jnp.int32, (CELLS, CIN), 0) % SIDE
    zero = jnp.zeros((SIDE, 3 * CIN), bf16)
    inner = pl.ds(SIDE, CELLS)
    for i, plane in enumerate(planes):
        wide[pl.ds(8, CELLS), :] = plane[...].astype(f32)
        taps[i, pl.ds(0, SIDE), :] = zero
        taps[i, pl.ds(SIDE + CELLS, SIDE), :] = zero
        left = jnp.where(col > 0, wide[pl.ds(7, CELLS), :], 0.0)
        right = jnp.where(col < SIDE - 1, wide[pl.ds(9, CELLS), :], 0.0)
        taps[i, inner, pl.ds(0, CIN)] = left.astype(bf16)
        taps[i, inner, pl.ds(CIN, CIN)] = plane[...]
        taps[i, inner, pl.ds(2 * CIN, CIN)] = right.astype(bf16)


def taps_scratch():
    return [pltpu.VMEM((CELLS + 16, CIN), f32), pltpu.VMEM((SLAB + 2, PADDED, 3 * CIN), bf16)]


def weight_grad_kernel(order, before, volume, after, cot, keep, send, wide, taps, turned):
    fill_taps((before, volume.at[0], volume.at[1], after), wide, taps)
    for j in range(SLAB * CELLS // 256):
        rows = pl.ds(j * 256, 256)
        turned[:, rows] = lax.dot_general(
            order[...], cot[rows, :], (((1,), (1,)), ((), ())), preferred_element_type=f32
        ).astype(bf16)
    for first in range(0, TAPS, 2):
        some = range(first, min(first + 2, TAPS))
        total = None
        for d in range(SLAB):
            parts = [
                taps[d + k // 9, pl.ds(k // 3 % 3 * SIDE, CELLS), pl.ds(k % 3 * CIN, CIN)] for k in some
            ]
            part = product(turned[:, pl.ds(d * CELLS, CELLS)], jnp.concatenate(parts, axis=1))
            total = part if total is None else total + part
        lanes = pl.ds(first * CIN, len(some) * CIN)
        keep[:, lanes] = total[: COUT // 2]
        send[:, lanes] = total[COUT // 2 :].astype(bf16)


def weight_grad_share(order, before, volume, after, cot):
    half = (COUT // 2, TAPS * CIN)
    return call(
        weight_grad_kernel,
        "weight_grad",
        (jax.ShapeDtypeStruct(half, f32), jax.ShapeDtypeStruct(half, bf16)),
        taps_scratch() + [pltpu.VMEM((COUT, SLAB * CELLS), bf16)],
        (order, before, volume, after, cot),
    )


def forward_kernel(before, volume, after, weight, out, wide, taps):
    fill_taps((before, volume.at[0], volume.at[1], after), wide, taps)
    for d in range(SLAB):

        def step(i, carry):
            base = pl.multiple_of(i * ROWS, ROWS)
            parts = [
                taps[
                    d + k // 9,
                    pl.ds(pl.multiple_of(base + k // 3 % 3 * SIDE, SIDE), ROWS),
                    pl.ds(k % 3 * CIN, CIN),
                ]
                for k in range(TAPS)
            ]
            pre = product(jnp.concatenate(parts, axis=1), weight[...])
            out[pl.ds(d * CELLS + base, ROWS), :] = jnp.where(pre >= 0, pre, 0.3 * pre).astype(bf16)
            return carry

        lax.fori_loop(0, CELLS // ROWS, step, 0)


def forward(before, volume, after, weight):
    return call(
        forward_kernel,
        "forward",
        jax.ShapeDtypeStruct((SLAB * CELLS, COUT), bf16),
        taps_scratch(),
        (before, volume, after, weight),
    )


def input_grad_kernel(before, cot, after, weight, out, padded, turned, sums):
    zero = jnp.zeros((SIDE, COUT), bf16)
    for i, plane in enumerate((before, cot.at[pl.ds(0, CELLS)], cot.at[pl.ds(CELLS, CELLS)], after)):
        padded[i, pl.ds(0, SIDE), :] = zero
        padded[i, pl.ds(SIDE + CELLS, SIDE), :] = zero
        padded[i, pl.ds(SIDE, CELLS), :] = plane[...]
    for k in range(TAPS):
        turned[pl.ds(k // 3 * COUT, COUT), pl.ds(k % 3 * CIN, CIN)] = weight[pl.ds(k * CIN, CIN), :].T
    col = lax.broadcasted_iota(jnp.int32, (ROWS, CIN), 0) % SIDE
    for d in range(SLAB):

        def step(i, carry):
            base = pl.multiple_of(i * ROWS, ROWS)
            parts = [
                padded[d + 2 - j // 3, pl.ds(pl.multiple_of(base + (2 - j % 3) * SIDE, SIDE), ROWS), :]
                for j in range(9)
            ]
            sums[pl.ds(8, ROWS), :] = product(jnp.concatenate(parts, axis=1), turned[...])
            total = sums[pl.ds(8, ROWS), pl.ds(CIN, CIN)]
            total = total + jnp.where(col < SIDE - 1, sums[pl.ds(9, ROWS), pl.ds(0, CIN)], 0.0)
            total = total + jnp.where(col > 0, sums[pl.ds(7, ROWS), pl.ds(2 * CIN, CIN)], 0.0)
            out[pl.ds(d * CELLS + base, ROWS), :] = total.astype(bf16)
            return carry

        lax.fori_loop(0, CELLS // ROWS, step, 0)


def input_grad_of(before, cot, after, weight):
    return call(
        input_grad_kernel,
        "input_grad",
        jax.ShapeDtypeStruct((SLAB * CELLS, CIN), bf16),
        [
            pltpu.VMEM((SLAB + 2, PADDED, COUT), bf16),
            pltpu.VMEM((9 * COUT, 3 * CIN), bf16),
            pltpu.VMEM((ROWS + 16, 3 * CIN), f32),
        ],
        (before, cot, after, weight),
    )


def neighbours(value, step):
    pairs = [(i, i + step) for i in range(16) if 0 <= i + step < 16]
    return lax.ppermute(value, "space", pairs)


def moved(x, y, z, c, bits):
    b = bits
    c = c ^ b[0]
    first, second = b[1] ^ (3 * b[3]), b[2] ^ (3 * b[4])
    x = x ^ (first + (second - first) * c)
    y = y ^ (second + (first - second) * c)
    return x, y, z ^ (b[5] + 2 * b[6] + 4 * b[7]), c


def partners(stage):
    bits = [int(i == stage) for i in range(8)]
    pairs = []
    for x in range(4):
        for y in range(4):
            for z in range(8):
                for c in range(2):
                    to = moved(x, y, z, c, bits)
                    pairs.append((x * 64 + y * 16 + z * 2 + c, to[0] * 64 + to[1] * 16 + to[2] * 2 + to[3]))
    return pairs


def row_order():
    dp, space = lax.axis_index("dp"), lax.axis_index("space")
    place = lax.iota(jnp.int32, COUT)
    bits = [place >> (7 - i) & 1 for i in range(8)]
    x, y, z, c = moved(dp // 4, dp % 4, space // 2, space % 2, bits)
    row = x * 64 + y * 16 + z * 2 + c
    return (row[:, None] == lax.iota(jnp.int32, COUT)[None, :]).astype(bf16)


def together(*arrays):
    return lax.optimization_barrier(arrays)


def swapped(send, stage):
    return lax.ppermute(send, ("dp", "space"), partners(stage))


def halved(keep, received, stage):
    total = keep + received.astype(f32)
    half = total.shape[0] // 2
    return total[:half], total[half:].astype(bf16 if stage < 5 else f32)


def shards(volume, weight, cotangent):
    volume = volume.reshape(SLAB, CELLS, CIN)
    cot = cotangent.reshape(SLAB * CELLS, COUT)
    weight = weight.reshape(TAPS * CIN, COUT)
    before, after = neighbours(volume[SLAB - 1], 1), neighbours(volume[0], -1)
    cot, before, after = together(cot, before, after)
    cot_before = neighbours(cot[(SLAB - 1) * CELLS :], 1)
    cot_after = neighbours(cot[:CELLS], -1)
    keep, send = weight_grad_share(row_order(), before, volume, after, cot)
    send, cot_before, cot_after = together(send, cot_before, cot_after)
    keep, send = halved(keep, swapped(send, 0), 0)

    received = swapped(send, 1)
    forward_weight, send = together(weight, send)
    activation = forward(before, volume, after, forward_weight)
    received, activation = together(received, activation)
    keep, send = halved(keep, received, 1)
    received = swapped(send, 2)
    back_weight, send = together(weight, send)
    input_grad = input_grad_of(cot_before, cot, cot_after, back_weight)
    received, input_grad = together(received, input_grad)

    for stage in range(2, 7):
        keep, send = halved(keep, received, stage)
        received = swapped(send, stage + 1)
    total = keep + received
    count = lax.axis_size("dp") * lax.axis_size("space") * SLAB * CELLS
    return (
        activation.reshape(1, SLAB, SIDE, SIDE, COUT),
        input_grad.reshape(1, SLAB, SIDE, SIDE, CIN),
        total / jnp.sqrt(f32(count)),
    )


def solution(mesh):
    slabs = P("dp", "space", None, None, None)
    return jax.shard_map(
        shards,
        mesh=mesh,
        in_specs=(slabs, P(), slabs),
        out_specs=(slabs, slabs, P(("dp", "space"), None)),
        check_vma=False,
    )
```

```python
import jax
import jax.numpy as jnp
from jax import lax
from jax.experimental import pallas as pl
from jax.experimental.pallas import tpu as pltpu
from jax.sharding import PartitionSpec as P

bf16, f32 = jnp.bfloat16, jnp.float32
SIDE = 32
CELLS = SIDE * SIDE
CIN, COUT, TAPS = 128, 256, 27
SLAB = 2
PADDED = CELLS + 2 * SIDE
ROWS = 1024
VMEM_LIMIT = 24 << 20
FLOPS = 2 * SLAB * CELLS * TAPS * CIN * COUT


def in_vmem():
    return pl.BlockSpec(memory_space=pltpu.VMEM)


def call(kernel, name, outs, scratch, args, flops):
    return pl.pallas_call(
        kernel,
        out_shape=outs,
        in_specs=[in_vmem()] * len(args),
        out_specs=tuple(in_vmem() for _ in outs),
        scratch_shapes=scratch,
        compiler_params=pltpu.CompilerParams(vmem_limit_bytes=VMEM_LIMIT),
        cost_estimate=pl.CostEstimate(flops=flops, bytes_accessed=4 << 20, transcendentals=0),
        name=name,
    )(*args)


def call_for_plane(kernel, name, d, lanes, scratch, args, earlier, flops):
    specs = [in_vmem()] * len(args)
    aliases = {}
    if earlier is not None:
        aliases = {len(args): 0}
        args, specs = (*args, earlier), specs + [pl.BlockSpec(memory_space=pl.ANY)]
    return pl.pallas_call(
        kernel,
        out_shape=jax.ShapeDtypeStruct((SLAB * CELLS, lanes), bf16),
        grid=(1,),
        in_specs=specs,
        out_specs=pl.BlockSpec((CELLS, lanes), lambda i: (d, 0)),
        scratch_shapes=scratch,
        input_output_aliases=aliases,
        compiler_params=pltpu.CompilerParams(vmem_limit_bytes=VMEM_LIMIT),
        cost_estimate=pl.CostEstimate(flops=flops, bytes_accessed=4 << 20, transcendentals=0),
        name=name,
    )(*args)


def product(a, b):
    return jnp.dot(a, b, preferred_element_type=f32)


def fill_taps(planes, wide, taps):
    col = lax.broadcasted_iota(jnp.int32, (CELLS, CIN), 0) % SIDE
    zero = jnp.zeros((SIDE, 3 * CIN), bf16)
    inner = pl.ds(SIDE, CELLS)
    for i, plane in enumerate(planes):
        wide[pl.ds(8, CELLS), :] = plane[...].astype(f32)
        taps[i, pl.ds(0, SIDE), :] = zero
        taps[i, pl.ds(SIDE + CELLS, SIDE), :] = zero
        left = jnp.where(col > 0, wide[pl.ds(7, CELLS), :], 0.0)
        right = jnp.where(col < SIDE - 1, wide[pl.ds(9, CELLS), :], 0.0)
        taps[i, inner, pl.ds(0, CIN)] = left.astype(bf16)
        taps[i, inner, pl.ds(CIN, CIN)] = plane[...]
        taps[i, inner, pl.ds(2 * CIN, CIN)] = right.astype(bf16)


WIDE = pltpu.VMEM((CELLS + 16, CIN), f32)
TAP_PLANES = jax.ShapeDtypeStruct((2, PADDED, 3 * CIN), bf16)


def taps_at(taps, plane, some):
    parts = [taps[plane, pl.ds(k // 3 % 3 * SIDE, CELLS), pl.ds(k % 3 * CIN, CIN)] for k in some]
    return jnp.concatenate(parts, axis=1)


def tap_groups(kd):
    return [range(k, min(k + 2, 9 * kd + 9)) for k in range(9 * kd, 9 * kd + 9, 2)]


def local_share_kernel(order, volume, cot, taps, turned, share, wide):
    fill_taps((volume.at[0], volume.at[1]), wide, taps)
    for j in range(SLAB * CELLS // 256):
        rows = pl.ds(j * 256, 256)
        turned[:, rows] = lax.dot_general(
            order[...], cot[rows, :], (((1,), (1,)), ((), ())), preferred_element_type=f32
        ).astype(bf16)
    for kd in range(3):
        for some in tap_groups(kd):
            total = None
            for d in range(SLAB):
                if 0 <= d + kd - 1 < SLAB:
                    part = product(turned[:, pl.ds(d * CELLS, CELLS)], taps_at(taps, d + kd - 1, some))
                    total = part if total is None else total + part
            share[:, pl.ds(some[0] * CIN, len(some) * CIN)] = total


def local_share(order, volume, cot):
    return call(
        local_share_kernel,
        "local_share",
        (
            TAP_PLANES,
            jax.ShapeDtypeStruct((COUT, SLAB * CELLS), bf16),
            jax.ShapeDtypeStruct((COUT, TAPS * CIN), f32),
        ),
        [WIDE],
        (order, volume, cot),
        FLOPS * 2 // 3,
    )


def edge_share_kernel(before, after, turned, share, taps, keep, send, wide):
    fill_taps((before, after), wide, taps)
    for kd in range(3):
        for some in tap_groups(kd):
            lanes = pl.ds(some[0] * CIN, len(some) * CIN)
            total = share[:, lanes]
            if kd != 1:
                edge = kd // 2
                total = total + product(turned[:, pl.ds(edge * CELLS, CELLS)], taps_at(taps, edge, some))
            keep[:, lanes] = total[: COUT // 2]
            send[:, lanes] = total[COUT // 2 :].astype(bf16)


def edge_share(before, after, turned, share):
    half = (COUT // 2, TAPS * CIN)
    return call(
        edge_share_kernel,
        "edge_share",
        (TAP_PLANES, jax.ShapeDtypeStruct(half, f32), jax.ShapeDtypeStruct(half, bf16)),
        [WIDE],
        (before, after, turned, share),
        FLOPS // 3,
    )


def forward(d, inner, outer, weight, earlier):
    def kernel(inner, outer, weight, *rest):
        out = rest[-1]
        planes = [(outer, 0), (inner, 0), (inner, 1), (outer, 1)][d : d + 3]

        def step(i, carry):
            base = pl.multiple_of(i * ROWS, ROWS)
            parts = []
            for k in range(TAPS):
                taps, plane = planes[k // 9]
                rows = pl.ds(pl.multiple_of(base + k // 3 % 3 * SIDE, SIDE), ROWS)
                parts.append(taps[plane, rows, pl.ds(k % 3 * CIN, CIN)])
            pre = product(jnp.concatenate(parts, axis=1), weight[...])
            out[pl.ds(base, ROWS), :] = jnp.where(pre >= 0, pre, 0.3 * pre).astype(bf16)
            return carry

        lax.fori_loop(0, CELLS // ROWS, step, 0)

    name = "forward_%d" % d
    return call_for_plane(kernel, name, d, COUT, [], (inner, outer, weight), earlier, FLOPS // 2)


def turn_weight_kernel(weight, turned):
    for k in range(TAPS):
        turned[pl.ds(k // 3 * COUT, COUT), pl.ds(k % 3 * CIN, CIN)] = weight[pl.ds(k * CIN, CIN), :].T


def turn_weight(weight):
    shape = jax.ShapeDtypeStruct((9 * COUT, 3 * CIN), bf16)
    return call(turn_weight_kernel, "turn_weight", (shape,), [], (weight,), 1 << 20)[0]


def input_grad_plane(d, before, cot, after, turned, earlier):
    def kernel(before, cot, after, turned, *rest):
        out, padded, sums = rest[-3:]
        zero = jnp.zeros((SIDE, COUT), bf16)
        planes = (before, cot.at[pl.ds(0, CELLS)], cot.at[pl.ds(CELLS, CELLS)], after)[d : d + 3]
        for i, plane in enumerate(planes):
            padded[i, pl.ds(0, SIDE), :] = zero
            padded[i, pl.ds(SIDE + CELLS, SIDE), :] = zero
            padded[i, pl.ds(SIDE, CELLS), :] = plane[...]
        col = lax.broadcasted_iota(jnp.int32, (ROWS, CIN), 0) % SIDE

        def step(i, carry):
            base = pl.multiple_of(i * ROWS, ROWS)
            parts = [
                padded[2 - j // 3, pl.ds(pl.multiple_of(base + (2 - j % 3) * SIDE, SIDE), ROWS), :]
                for j in range(9)
            ]
            sums[pl.ds(8, ROWS), :] = product(jnp.concatenate(parts, axis=1), turned[...])
            total = sums[pl.ds(8, ROWS), pl.ds(CIN, CIN)]
            total = total + jnp.where(col < SIDE - 1, sums[pl.ds(9, ROWS), pl.ds(0, CIN)], 0.0)
            total = total + jnp.where(col > 0, sums[pl.ds(7, ROWS), pl.ds(2 * CIN, CIN)], 0.0)
            out[pl.ds(base, ROWS), :] = total.astype(bf16)
            return carry

        lax.fori_loop(0, CELLS // ROWS, step, 0)

    scratch = [pltpu.VMEM((3, PADDED, COUT), bf16), pltpu.VMEM((ROWS + 16, 3 * CIN), f32)]
    name = "input_grad_%d" % d
    return call_for_plane(kernel, name, d, CIN, scratch, (before, cot, after, turned), earlier, FLOPS // 2)


def neighbours(value, step):
    pairs = [(i, i + step) for i in range(16) if 0 <= i + step < 16]
    return lax.ppermute(value, "space", pairs)


def moved(x, y, z, c, bits):
    b = bits
    c = c ^ b[0]
    first, second = b[1] ^ (3 * b[3]), b[2] ^ (3 * b[4])
    x = x ^ (first + (second - first) * c)
    y = y ^ (second + (first - second) * c)
    even = lambda z: z ^ 1
    odd = lambda z: ((z + 1) % 8 ^ 1) + 7 & 7
    z = z + (even(z) - z) * b[5]
    z = z + (odd(z) - z) * b[6]
    z = z + (even(odd(even(z))) - z) * b[7]
    return x, y, z, c


def partners(stage):
    bits = [int(i == stage) for i in range(8)]
    pairs = []
    for x in range(4):
        for y in range(4):
            for z in range(8):
                for c in range(2):
                    to = moved(x, y, z, c, bits)
                    pairs.append((x * 64 + y * 16 + z * 2 + c, to[0] * 64 + to[1] * 16 + to[2] * 2 + to[3]))
    return pairs


def row_order():
    dp, space = lax.axis_index("dp"), lax.axis_index("space")
    place = lax.iota(jnp.int32, COUT)
    bits = [place >> (7 - i) & 1 for i in range(8)]
    x, y, z, c = moved(dp // 4, dp % 4, space // 2, space % 2, bits)
    row = x * 64 + y * 16 + z * 2 + c
    return (row[:, None] == lax.iota(jnp.int32, COUT)[None, :]).astype(bf16)


def together(*arrays):
    return lax.optimization_barrier(arrays)


def swapped(send, stage):
    return lax.ppermute(send, ("dp", "space"), partners(stage))


def halved(keep, received, stage):
    total = keep + received.astype(f32)
    half = total.shape[0] // 2
    return total[:half], total[half:].astype(bf16 if stage < 5 else f32)


def shards(volume, weight, cotangent):
    volume = volume.reshape(SLAB, CELLS, CIN)
    cot = cotangent.reshape(SLAB * CELLS, COUT)
    weight = weight.reshape(TAPS * CIN, COUT)

    before, after = neighbours(volume[SLAB - 1], 1), neighbours(volume[0], -1)
    inner, turned, share = local_share(row_order(), volume, cot)
    before, after, inner, turned, share = together(before, after, inner, turned, share)
    outer, keep, send = edge_share(before, after, turned, share)

    received = swapped(send, 0)
    weight, send = together(weight, send)
    back_weight = turn_weight(weight)
    received, back_weight = together(received, back_weight)
    keep, send = halved(keep, received, 0)

    received = swapped(send, 1)
    weight, send = together(weight, send)
    activation = forward(0, inner, outer, weight, None)
    cot, activation = together(cot, activation)
    cot_before = neighbours(cot[(SLAB - 1) * CELLS :], 1)
    cot_after = neighbours(cot[:CELLS], -1)
    received, activation = together(received, activation)
    keep, send = halved(keep, received, 1)

    received = swapped(send, 2)
    weight, send = together(weight, send)
    activation = forward(1, inner, outer, weight, activation)
    received, activation, cot_before, cot_after = together(received, activation, cot_before, cot_after)
    keep, send = halved(keep, received, 2)

    received = swapped(send, 3)
    back_weight, send = together(back_weight, send)
    input_grad = input_grad_plane(0, cot_before, cot, cot_after, back_weight, None)
    received, input_grad = together(received, input_grad)
    keep, send = halved(keep, received, 3)

    received = swapped(send, 4)
    back_weight, send = together(back_weight, send)
    input_grad = input_grad_plane(1, cot_before, cot, cot_after, back_weight, input_grad)
    received, input_grad = together(received, input_grad)

    for stage in range(4, 7):
        keep, send = halved(keep, received, stage)
        received = swapped(send, stage + 1)
    total = keep + received
    count = lax.axis_size("dp") * lax.axis_size("space") * SLAB * CELLS
    return (
        activation.reshape(1, SLAB, SIDE, SIDE, COUT),
        input_grad.reshape(1, SLAB, SIDE, SIDE, CIN),
        total / jnp.sqrt(f32(count)),
    )


def solution(mesh):
    slabs = P("dp", "space", None, None, None)
    return jax.shard_map(
        shards,
        mesh=mesh,
        in_specs=(slabs, P(), slabs),
        out_specs=(slabs, slabs, P(("dp", "space"), None)),
        check_vma=False,
    )
```

```python
import jax
import jax.numpy as jnp
from jax import lax
from jax.experimental import pallas as pl
from jax.experimental.pallas import tpu as pltpu
from jax.sharding import PartitionSpec as P

bf16, f32 = jnp.bfloat16, jnp.float32
SIDE = 32
CELLS = SIDE * SIDE
CIN, COUT, TAPS = 128, 256, 27
SLAB = 2
PADDED = CELLS + 2 * SIDE
COLUMNS = TAPS * CIN
VMEM_SOME, VMEM_MOST = 24 << 20, 58 << 20
FLOPS = 2 * SLAB * CELLS * TAPS * CIN * COUT

IN_VMEM = pl.BlockSpec(memory_space=pltpu.VMEM)
IN_SMEM = pl.BlockSpec(memory_space=pltpu.SMEM)
IN_HBM = pl.BlockSpec(memory_space=pltpu.HBM)


def shaped(kind, *shape):
    return jax.ShapeDtypeStruct(shape, kind)


def call(kernel, outs, args, scratch=(), flops=1 << 20, specs=None, vmem=VMEM_SOME, **options):
    if specs is None:
        specs = [IN_VMEM if a.ndim > 1 else IN_SMEM for a in args]
    options.setdefault("out_specs", tuple(IN_VMEM for _ in outs))
    return pl.pallas_call(
        kernel,
        out_shape=outs,
        in_specs=specs,
        scratch_shapes=list(scratch),
        compiler_params=pltpu.CompilerParams(vmem_limit_bytes=vmem),
        cost_estimate=pl.CostEstimate(flops=flops, bytes_accessed=4 << 20, transcendentals=0),
        **options,
    )(*args)


def product(a, b):
    return jnp.dot(a, b, preferred_element_type=f32)


def fill_taps(plane, i, wide, taps):
    col = lax.broadcasted_iota(jnp.int32, (CELLS, CIN), 0) % SIDE
    zero = jnp.zeros((SIDE, 3 * CIN), bf16)
    inner = pl.ds(SIDE, CELLS)
    wide[pl.ds(8, CELLS), :] = plane[...].astype(f32)
    taps[i, pl.ds(0, SIDE), :] = zero
    taps[i, pl.ds(SIDE + CELLS, SIDE), :] = zero
    left = jnp.where(col > 0, wide[pl.ds(7, CELLS), :], 0.0)
    right = jnp.where(col < SIDE - 1, wide[pl.ds(9, CELLS), :], 0.0)
    taps[i, inner, pl.ds(0, CIN)] = left.astype(bf16)
    taps[i, inner, pl.ds(CIN, CIN)] = plane[...]
    taps[i, inner, pl.ds(2 * CIN, CIN)] = right.astype(bf16)


def taps_scratch(planes):
    return [pltpu.VMEM((CELLS + 16, CIN), f32), pltpu.VMEM((planes, PADDED, 3 * CIN), bf16)]


def taps_at(taps, plane, some):
    parts = [taps[plane, pl.ds(k // 3 % 3 * SIDE, CELLS), pl.ds(k % 3 * CIN, CIN)] for k in some]
    return jnp.concatenate(parts, axis=1)


def tap_groups(kd):
    return [range(k, min(k + 2, 9 * kd + 9)) for k in range(9 * kd, 9 * kd + 9, 2)]


def local_share_kernel(core, order, volume, cot, cot_near, cot_far, turned, share, wide, taps):
    c = core[0]
    cot_near[...] = cot[pl.ds(pl.multiple_of((1 - c) * CELLS, CELLS), CELLS), :]
    cot_far[...] = cot[pl.ds(pl.multiple_of(c * CELLS, CELLS), CELLS), :]
    for i in range(SLAB):
        fill_taps(volume.at[i], i, wide, taps)
    for j in range(SLAB * CELLS // 256):
        rows = pl.ds(j * 256, 256)
        turned[:, rows] = lax.dot_general(
            order[...], cot[rows, :], (((1,), (1,)), ((), ())), preferred_element_type=f32
        ).astype(bf16)
    for kd in range(3):
        for some in tap_groups(kd):
            total = None
            for d in range(SLAB):
                if 0 <= d + kd - 1 < SLAB:
                    part = product(turned[:, pl.ds(d * CELLS, CELLS)], taps_at(taps, d + kd - 1, some))
                    total = part if total is None else total + part
            share[:, pl.ds(some[0] * CIN, len(some) * CIN)] = total


def local_share(*args):
    plane = shaped(bf16, CELLS, COUT)
    outs = (plane, plane, shaped(bf16, COUT, SLAB * CELLS), shaped(f32, COUT, COLUMNS))
    return call(local_share_kernel, outs, args, taps_scratch(2), FLOPS * 2 // 3, name="local_share")


def edge_share_kernel(core, near, far, turned, share, keep, send, wide, taps):
    c = core[0]
    fill_taps(near, 1 - c, wide, taps)
    fill_taps(far, c, wide, taps)
    for kd in range(3):
        for some in tap_groups(kd):
            lanes = pl.ds(some[0] * CIN, len(some) * CIN)
            total = share[:, lanes]
            if kd != 1:
                edge = kd // 2
                total = total + product(turned[:, pl.ds(edge * CELLS, CELLS)], taps_at(taps, edge, some))
            keep[:, lanes] = total[: COUT // 2]
            send[:, lanes] = total[COUT // 2 :].astype(bf16)


def edge_share(core, near, far, turned, share):
    outs = (shaped(f32, COUT // 2, COLUMNS), shaped(bf16, COUT // 2, COLUMNS))
    args = (core, near, far, turned, share)
    return call(edge_share_kernel, outs, args, taps_scratch(2), FLOPS // 3, name="edge_share")


def forward_kernel(core, near, volume, far, weight, out, wide, taps):
    c = core[0]
    step = pl.program_id(0)

    @pl.when(step == 0)
    def _():
        for i in range(SLAB):
            fill_taps(volume.at[i], 1 + i, wide, taps)
        fill_taps(near, 3 * (1 - c), wide, taps)
        fill_taps(far, 3 * c, wide, taps)

    parts = []
    for k in range(TAPS):
        parts.append(taps[step + k // 9, pl.ds(k // 3 % 3 * SIDE, CELLS), pl.ds(k % 3 * CIN, CIN)])
    pre = product(jnp.concatenate(parts, axis=1), weight[...])
    out[...] = jnp.where(pre >= 0, pre, 0.3 * pre).astype(bf16)


def forward(*args):
    return call(
        forward_kernel,
        (shaped(bf16, SLAB * CELLS, COUT),),
        args,
        taps_scratch(4),
        FLOPS,
        grid=(SLAB,),
        out_specs=(pl.BlockSpec((CELLS, COUT), lambda i: (i, 0)),),
        vmem=VMEM_MOST,
        name="forward",
    )[0]


def turn_weight_kernel(weight, turned):
    for k in range(TAPS):
        turned[pl.ds(k // 3 * COUT, COUT), pl.ds(k % 3 * CIN, CIN)] = weight[pl.ds(k * CIN, CIN), :].T


def turn_weight(weight):
    return call(turn_weight_kernel, (shaped(bf16, 9 * COUT, 3 * CIN),), (weight,), name="turn_weight")[0]


def input_grad_kernel(core, near, cot, far, turned, out, padded, sums):
    c = core[0]
    step = pl.program_id(0)
    middle = pl.ds(SIDE, CELLS)

    @pl.when(step == 0)
    def _():
        zero = jnp.zeros((SIDE, COUT), bf16)
        for i in range(4):
            padded[i, pl.ds(0, SIDE), :] = zero
            padded[i, pl.ds(SIDE + CELLS, SIDE), :] = zero
        for i in range(SLAB):
            padded[1 + i, middle, :] = cot[pl.ds(i * CELLS, CELLS), :]
        padded[3 * (1 - c), middle, :] = near[...]
        padded[3 * c, middle, :] = far[...]

    parts = [padded[step + 2 - j // 3, pl.ds((2 - j % 3) * SIDE, CELLS), :] for j in range(9)]
    sums[pl.ds(8, CELLS), :] = product(jnp.concatenate(parts, axis=1), turned[...])
    col = lax.broadcasted_iota(jnp.int32, (CELLS, CIN), 0) % SIDE
    total = sums[pl.ds(8, CELLS), pl.ds(CIN, CIN)]
    total = total + jnp.where(col < SIDE - 1, sums[pl.ds(9, CELLS), pl.ds(0, CIN)], 0.0)
    total = total + jnp.where(col > 0, sums[pl.ds(7, CELLS), pl.ds(2 * CIN, CIN)], 0.0)
    out[...] = total.astype(bf16)


def input_grad_of(*args):
    return call(
        input_grad_kernel,
        (shaped(bf16, SLAB * CELLS, CIN),),
        args,
        [pltpu.VMEM((4, PADDED, COUT), bf16), pltpu.VMEM((CELLS + 16, 3 * CIN), f32)],
        FLOPS,
        grid=(SLAB,),
        out_specs=(pl.BlockSpec((CELLS, CIN), lambda i: (i, 0)),),
        vmem=VMEM_MOST,
        name="input_grad",
    )[0]


def from_core(value):
    return lax.ppermute(value, "space", [(i, i ^ 1) for i in range(16)])


def from_chip(value):
    return lax.ppermute(value, "space", [(i, ((i + 1) ^ 1) - 1) for i in range(1, 15)])


def row_order(core):
    place = lax.iota(jnp.int32, COUT)
    row = (place & 127) * 2 + (core ^ (place >> 7))
    return (row[:, None] == lax.iota(jnp.int32, COUT)[None, :]).astype(bf16)


def together(*arrays):
    return lax.optimization_barrier(arrays)


def shards(volume, weight, cotangent):
    volume = volume.reshape(SLAB, CELLS, CIN)
    cot = cotangent.reshape(SLAB * CELLS, COUT)
    weight = weight.reshape(COLUMNS, COUT)
    core = lax.axis_index("space").astype(jnp.int32) % 2
    flag = core.reshape(1)

    def plane(i):
        return lax.dynamic_index_in_dim(volume, i, 0, False)

    far, near = from_chip(plane(core)), from_core(plane(1 - core))
    cot_near, cot_far, turned, share = local_share(flag, row_order(core), volume, cot)
    far, near, turned, share = together(far, near, turned, share)
    keep, send = edge_share(flag, near, far, turned, share)

    received = from_core(send)
    weight, send = together(weight, send)
    back_weight = turn_weight(weight)
    cot_far, cot_near, back_weight = together(cot_far, cot_near, back_weight)
    cot_far, cot_near = from_chip(cot_far), from_core(cot_near)
    received, back_weight = together(received, back_weight)
    total = keep + received.astype(f32)

    dp = lax.axis_size("dp")
    send = total.astype(bf16).reshape(dp, -1, COLUMNS)
    parts = lax.all_to_all(send, "dp", 0, 0)
    weight, send = together(weight, send)
    activation = forward(flag, near, volume, far, weight)
    parts, activation = together(parts, activation)
    send = jnp.sum(parts.astype(f32), axis=0).reshape(8, 1, COLUMNS)

    parts = lax.all_to_all(send, "space", 0, 0, axis_index_groups=[list(range(c, 16, 2)) for c in range(2)])
    back_weight, send = together(back_weight, send)
    input_grad = input_grad_of(flag, cot_near, cot, cot_far, back_weight)
    parts, input_grad = together(parts, input_grad)
    count = dp * lax.axis_size("space") * SLAB * CELLS
    return (
        activation.reshape(1, SLAB, SIDE, SIDE, COUT),
        input_grad.reshape(1, SLAB, SIDE, SIDE, CIN),
        jnp.sum(parts, axis=0) / jnp.sqrt(f32(count)),
    )


def solution(mesh):
    slabs = P("dp", "space", None, None, None)
    return jax.shard_map(
        shards,
        mesh=mesh,
        in_specs=(slabs, P(), slabs),
        out_specs=(slabs, slabs, P(("dp", "space"), None)),
        check_vma=False,
    )
```

```python
import functools

import jax
import jax.numpy as jnp
from jax import lax
from jax.experimental import pallas as pl
from jax.experimental.pallas import tpu as pltpu
from jax.sharding import PartitionSpec as P

bf16, f32 = jnp.bfloat16, jnp.float32
SIDE = 32
CELLS = SIDE * SIDE
CIN, COUT, TAPS = 128, 256, 27
SLAB = 2
PADDED = CELLS + 2 * SIDE
COLUMNS = TAPS * CIN
VMEM_SOME, VMEM_MORE, VMEM_MOST = 24 << 20, 55_000_000, 63_400_000
FLOPS = 2 * SLAB * CELLS * TAPS * CIN * COUT

IN_VMEM = pl.BlockSpec(memory_space=pltpu.VMEM)
IN_SMEM = pl.BlockSpec(memory_space=pltpu.SMEM)
IN_HBM = pl.BlockSpec(memory_space=pltpu.HBM)


def shaped(kind, *shape):
    return jax.ShapeDtypeStruct(shape, kind)


def call(kernel, outs, args, scratch=(), flops=1 << 20, specs=None, vmem=VMEM_SOME, **options):
    if specs is None:
        specs = [IN_VMEM if a.ndim > 1 else IN_SMEM for a in args]
    options.setdefault("out_specs", tuple(IN_VMEM for _ in outs))
    return pl.pallas_call(
        kernel,
        out_shape=outs,
        in_specs=specs,
        scratch_shapes=list(scratch),
        compiler_params=pltpu.CompilerParams(vmem_limit_bytes=vmem),
        cost_estimate=pl.CostEstimate(flops=flops, bytes_accessed=4 << 20, transcendentals=0),
        **options,
    )(*args)


def product(a, b):
    return jnp.dot(a, b, preferred_element_type=f32)


def fill_taps(plane, i, wide, taps):
    col = lax.broadcasted_iota(jnp.int32, (CELLS, CIN), 0) % SIDE
    zero = jnp.zeros((SIDE, 3 * CIN), bf16)
    inner = pl.ds(SIDE, CELLS)
    wide[pl.ds(8, CELLS), :] = plane[...].astype(f32)
    taps[i, pl.ds(0, SIDE), :] = zero
    taps[i, pl.ds(SIDE + CELLS, SIDE), :] = zero
    left = jnp.where(col > 0, wide[pl.ds(7, CELLS), :], 0.0)
    right = jnp.where(col < SIDE - 1, wide[pl.ds(9, CELLS), :], 0.0)
    taps[i, inner, pl.ds(0, CIN)] = left.astype(bf16)
    taps[i, inner, pl.ds(CIN, CIN)] = plane[...]
    taps[i, inner, pl.ds(2 * CIN, CIN)] = right.astype(bf16)


def taps_scratch(planes):
    return [pltpu.VMEM((CELLS + 16, CIN), f32), pltpu.VMEM((planes, PADDED, 3 * CIN), bf16)]


def taps_at(taps, plane, some):
    parts = [taps[plane, pl.ds(k // 3 % 3 * SIDE, CELLS), pl.ds(k % 3 * CIN, CIN)] for k in some]
    return jnp.concatenate(parts, axis=1)


def tap_groups(kd):
    return [range(k, min(k + 2, 9 * kd + 9)) for k in range(9 * kd, 9 * kd + 9, 2)]


def local_share_kernel(core, order, volume, cot, cot_near, cot_far, turned, share, wide, taps):
    c = core[0]
    cot_near[...] = cot[pl.ds(pl.multiple_of((1 - c) * CELLS, CELLS), CELLS), :]
    cot_far[...] = cot[pl.ds(pl.multiple_of(c * CELLS, CELLS), CELLS), :]
    for i in range(SLAB):
        fill_taps(volume.at[i], i, wide, taps)
    for j in range(SLAB * CELLS // 256):
        rows = pl.ds(j * 256, 256)
        turned[:, rows] = lax.dot_general(
            order[...], cot[rows, :], (((1,), (1,)), ((), ())), preferred_element_type=f32
        ).astype(bf16)
    for kd in range(3):
        for some in tap_groups(kd):
            total = None
            for d in range(SLAB):
                if 0 <= d + kd - 1 < SLAB:
                    part = product(turned[:, pl.ds(d * CELLS, CELLS)], taps_at(taps, d + kd - 1, some))
                    total = part if total is None else total + part
            share[:, pl.ds(some[0] * CIN, len(some) * CIN)] = total


def local_share(*args):
    plane = shaped(bf16, CELLS, COUT)
    outs = (plane, plane, shaped(bf16, COUT, SLAB * CELLS), shaped(f32, COUT, COLUMNS))
    return call(local_share_kernel, outs, args, taps_scratch(2), FLOPS * 2 // 3, name="local_share")


def edge_share_kernel(core, near, far, turned, share, keep, send, wide, taps):
    c = core[0]
    fill_taps(near, 1 - c, wide, taps)
    fill_taps(far, c, wide, taps)
    for kd in range(3):
        for some in tap_groups(kd):
            lanes = pl.ds(some[0] * CIN, len(some) * CIN)
            total = share[:, lanes]
            if kd != 1:
                edge = kd // 2
                total = total + product(turned[:, pl.ds(edge * CELLS, CELLS)], taps_at(taps, edge, some))
            keep[:, lanes] = total[: COUT // 2]
            send[:, lanes] = total[COUT // 2 :].astype(bf16)


def edge_share(core, near, far, turned, share):
    outs = (shaped(f32, COUT // 2, COLUMNS), shaped(bf16, COUT // 2, COLUMNS))
    args = (core, near, far, turned, share)
    return call(edge_share_kernel, outs, args, taps_scratch(2), FLOPS // 3, name="edge_share")


def start_all(pairs, sems):
    copies = [pltpu.make_async_copy(source, target, sems.at[i]) for i, (source, target) in enumerate(pairs)]
    for copy in copies:
        copy.start()
    return copies


def forward_kernel(core, near, volume, far, weight_in_hbm, out, wide, taps, planes, weight, sems):
    c = core[0]
    step = pl.program_id(0)

    @pl.when(step == 0)
    def _():
        own, *outer, whole = start_all(
            [(volume, planes.at[pl.ds(0, SLAB)]), (near, planes.at[2]), (far, planes.at[3]), (weight_in_hbm, weight)],
            sems,
        )
        own.wait()
        for i in range(SLAB):
            fill_taps(planes.at[i], 1 + i, wide, taps)
        for copy in outer:
            copy.wait()
        fill_taps(planes.at[2], 3 * (1 - c), wide, taps)
        fill_taps(planes.at[3], 3 * c, wide, taps)
        whole.wait()

    parts = []
    for k in range(TAPS):
        parts.append(taps[step + k // 9, pl.ds(k // 3 % 3 * SIDE, CELLS), pl.ds(k % 3 * CIN, CIN)])
    pre = product(jnp.concatenate(parts, axis=1), weight[...])
    out[...] = jnp.where(pre >= 0, pre, 0.3 * pre).astype(bf16)


def forward(*args):
    own_copies = [
        pltpu.VMEM((4, CELLS, CIN), bf16),
        pltpu.VMEM((COLUMNS, COUT), bf16),
        pltpu.SemaphoreType.DMA((4,)),
    ]
    return call(
        forward_kernel,
        (shaped(bf16, SLAB * CELLS, COUT),),
        args,
        taps_scratch(4) + own_copies,
        FLOPS,
        specs=[IN_SMEM] + [IN_HBM] * 4,
        grid=(SLAB,),
        out_specs=(pl.BlockSpec((CELLS, COUT), lambda i: (i, 0)),),
        vmem=VMEM_MOST,
        name="forward",
    )[0]


def sum_rows_kernel(parts, rows, spread):
    total = parts[0].astype(f32)
    for i in range(1, parts.shape[0]):
        total = total + parts[i].astype(f32)
    for k in range(TAPS):
        spread[:, k, :] = total[:, k * CIN : (k + 1) * CIN]
    rows[...] = spread[...].astype(bf16)


def sum_rows(parts):
    shape = (parts.shape[1], TAPS, CIN)
    return call(sum_rows_kernel, (shaped(bf16, *shape),), (parts,), [pltpu.VMEM(shape, f32)], name="sum_rows")[0]


def finish(parts, count):
    def kernel(parts, row):
        total = jnp.sum(parts[...].astype(f32), axis=0) / jnp.sqrt(f32(count))
        for k in range(TAPS):
            row[:, pl.ds(k * CIN, CIN)] = total[k : k + 1, :]

    return call(kernel, (shaped(f32, 1, COLUMNS),), (parts,), name="finish")[0]


def turn_weight_kernel(weight, turned):
    for k in range(TAPS):
        turned[pl.ds(k // 3 * COUT, COUT), pl.ds(k % 3 * CIN, CIN)] = weight[pl.ds(k * CIN, CIN), :].T


def turn_weight(weight):
    return call(turn_weight_kernel, (shaped(bf16, 9 * COUT, 3 * CIN),), (weight,), name="turn_weight")[0]


def input_grad_kernel(is_far, core, halo, cot, turned, *rest):
    out, padded, weight, sums, result, sems = rest[-6:]
    d = core[0] if is_far else 1 - core[0]
    middle = pl.ds(SIDE, CELLS)
    planes = [
        cot.at[pl.ds(pl.multiple_of(d * CELLS, CELLS), CELLS)],
        cot.at[pl.ds(pl.multiple_of((1 - d) * CELLS, CELLS), CELLS)],
        halo,
    ]
    pairs = []
    for slot, kd in enumerate((1, 2 * d, 2 - 2 * d)):
        rows = pl.ds(pl.multiple_of(kd * 3 * COUT, 3 * COUT), 3 * COUT)
        pairs += [(planes[slot], padded.at[slot, middle]), (turned.at[rows], weight.at[slot])]
    copies = start_all(pairs, sems)
    zero = jnp.zeros((SIDE, COUT), bf16)
    inner = pl.ds(8, CELLS)
    for slot in range(3):
        padded[slot, pl.ds(0, SIDE), :] = zero
        padded[slot, pl.ds(SIDE + CELLS, SIDE), :] = zero
        for copy in copies[2 * slot : 2 * slot + 2]:
            copy.wait()
        parts = [padded[slot, pl.ds((2 - kh) * SIDE, CELLS), :] for kh in range(3)]
        part = product(jnp.concatenate(parts, axis=1), weight[slot])
        sums[inner, :] = part if slot == 0 else sums[inner, :] + part
    col = lax.broadcasted_iota(jnp.int32, (CELLS, CIN), 0) % SIDE
    total = sums[inner, pl.ds(CIN, CIN)]
    total = total + jnp.where(col < SIDE - 1, sums[pl.ds(9, CELLS), pl.ds(0, CIN)], 0.0)
    total = total + jnp.where(col > 0, sums[pl.ds(7, CELLS), pl.ds(2 * CIN, CIN)], 0.0)
    result[...] = total.astype(bf16)
    write = pltpu.make_async_copy(result, out.at[pl.ds(pl.multiple_of(d * CELLS, CELLS), CELLS)], sems.at[6])
    write.start()
    write.wait()


def input_grad_plane(is_far, *args):
    scratch = [
        pltpu.VMEM((3, PADDED, COUT), bf16),
        pltpu.VMEM((3, 3 * COUT, 3 * CIN), bf16),
        pltpu.VMEM((CELLS + 16, 3 * CIN), f32),
        pltpu.VMEM((CELLS, CIN), bf16),
        pltpu.SemaphoreType.DMA((7,)),
    ]
    return call(
        functools.partial(input_grad_kernel, is_far),
        (shaped(bf16, SLAB * CELLS, CIN),),
        args,
        scratch,
        FLOPS // 2,
        specs=[IN_SMEM] + [IN_HBM] * (len(args) - 1),
        out_specs=(IN_HBM,),
        input_output_aliases={4: 0} if len(args) > 4 else {},
        vmem=VMEM_MORE,
        name="input_grad_far" if is_far else "input_grad_near",
    )[0]


def from_core(value):
    return lax.ppermute(value, "space", [(i, i ^ 1) for i in range(16)])


def from_chip(value):
    return lax.ppermute(value, "space", [(i, ((i + 1) ^ 1) - 1) for i in range(1, 15)])


def row_order_kernel(core, order):
    place = lax.broadcasted_iota(jnp.int32, (COUT, COUT), 0)
    row = (place & 127) * 2 + (core[0] ^ (place >> 7))
    order[...] = jnp.where(row == lax.broadcasted_iota(jnp.int32, (COUT, COUT), 1), 1.0, 0.0).astype(bf16)


def row_order(core):
    return call(row_order_kernel, (shaped(bf16, COUT, COUT),), (core,), flops=FLOPS, name="row_order")[0]


def together(*arrays):
    return lax.optimization_barrier(arrays)


def shards(volume, weight, cotangent):
    volume = volume.reshape(SLAB, CELLS, CIN)
    cot = cotangent.reshape(SLAB * CELLS, COUT)
    weight = weight.reshape(COLUMNS, COUT)
    core = lax.axis_index("space").astype(jnp.int32) % 2
    flag = core.reshape(1)

    def plane(i):
        return lax.dynamic_index_in_dim(volume, i, 0, False)

    far, near, order = together(plane(core), plane(1 - core), row_order(flag))
    far, near = from_chip(far), from_core(near)
    cot_near, cot_far, turned, share = local_share(flag, order, volume, cot)
    far, near, turned, share = together(far, near, turned, share)
    keep, send = edge_share(flag, near, far, turned, share)

    received = from_core(send)
    weight, send = together(weight, send)
    back_weight = turn_weight(weight)
    cot_far, cot_near, back_weight = together(cot_far, cot_near, back_weight)
    cot_far, cot_near = from_chip(cot_far), from_core(cot_near)
    received, back_weight = together(received, back_weight)
    total = keep + received.astype(f32)

    dp = lax.axis_size("dp")
    send = total.astype(bf16).reshape(dp, -1, COLUMNS)
    parts = lax.all_to_all(send, "dp", 0, 0)
    weight, send = together(weight, send)
    activation = forward(flag, near, volume, far, weight)
    back_weight, activation = together(back_weight, activation)
    input_grad = input_grad_plane(False, flag, cot_near, cot, back_weight)
    parts, input_grad = together(parts, input_grad)
    send = sum_rows(parts)

    parts = lax.all_to_all(send, "space", 0, 0, axis_index_groups=[list(range(c, 16, 2)) for c in range(2)])
    back_weight, send = together(back_weight, send)
    input_grad = input_grad_plane(True, flag, cot_far, cot, back_weight, input_grad)
    parts, input_grad = together(parts, input_grad)
    count = dp * lax.axis_size("space") * SLAB * CELLS
    return (
        activation.reshape(1, SLAB, SIDE, SIDE, COUT),
        input_grad.reshape(1, SLAB, SIDE, SIDE, CIN),
        finish(parts, count),
    )


def solution(mesh):
    slabs = P("dp", "space", None, None, None)
    return jax.shard_map(
        shards,
        mesh=mesh,
        in_specs=(slabs, P(), slabs),
        out_specs=(slabs, slabs, P(("dp", "space"), None)),
        check_vma=False,
    )
```

```python
import functools

import jax
import jax.numpy as jnp
from jax import lax
from jax.experimental import pallas as pl
from jax.experimental.pallas import tpu as pltpu
from jax.sharding import PartitionSpec as P

bf16, f32 = jnp.bfloat16, jnp.float32
SIDE = 32
CELLS = SIDE * SIDE
CIN, COUT, TAPS = 128, 256, 27
SLAB = 2
PADDED = CELLS + 2 * SIDE
COLUMNS = TAPS * CIN
VMEM_SOME, VMEM_MORE, VMEM_MOST = 24 << 20, 55_000_000, 63_400_000
FLOPS = 2 * SLAB * CELLS * TAPS * CIN * COUT

IN_VMEM = pl.BlockSpec(memory_space=pltpu.VMEM)
IN_SMEM = pl.BlockSpec(memory_space=pltpu.SMEM)
IN_HBM = pl.BlockSpec(memory_space=pltpu.HBM)


def shaped(kind, *shape):
    return jax.ShapeDtypeStruct(shape, kind)


def call(kernel, outs, args, scratch=(), flops=1 << 20, specs=None, vmem=VMEM_SOME, **options):
    if specs is None:
        specs = [IN_VMEM if a.ndim > 1 else IN_SMEM for a in args]
    options.setdefault("out_specs", tuple(IN_VMEM for _ in outs))
    return pl.pallas_call(
        kernel,
        out_shape=outs,
        in_specs=specs,
        scratch_shapes=list(scratch),
        compiler_params=pltpu.CompilerParams(vmem_limit_bytes=vmem),
        cost_estimate=pl.CostEstimate(flops=flops, bytes_accessed=4 << 20, transcendentals=0),
        **options,
    )(*args)


def product(a, b):
    return jnp.dot(a, b, preferred_element_type=f32)


def fill_taps(plane, i, wide, taps):
    col = lax.broadcasted_iota(jnp.int32, (CELLS, CIN), 0) % SIDE
    zero = jnp.zeros((SIDE, 3 * CIN), bf16)
    inner = pl.ds(SIDE, CELLS)
    wide[pl.ds(8, CELLS), :] = plane[...].astype(f32)
    taps[i, pl.ds(0, SIDE), :] = zero
    taps[i, pl.ds(SIDE + CELLS, SIDE), :] = zero
    left = jnp.where(col > 0, wide[pl.ds(7, CELLS), :], 0.0)
    right = jnp.where(col < SIDE - 1, wide[pl.ds(9, CELLS), :], 0.0)
    taps[i, inner, pl.ds(0, CIN)] = left.astype(bf16)
    taps[i, inner, pl.ds(CIN, CIN)] = plane[...]
    taps[i, inner, pl.ds(2 * CIN, CIN)] = right.astype(bf16)


def taps_scratch(planes):
    return [pltpu.VMEM((CELLS + 16, CIN), f32), pltpu.VMEM((planes, PADDED, 3 * CIN), bf16)]


def taps_at(taps, plane, some):
    parts = [taps[plane, pl.ds(k // 3 % 3 * SIDE, CELLS), pl.ds(k % 3 * CIN, CIN)] for k in some]
    return jnp.concatenate(parts, axis=1)


def tap_groups(kd):
    return [range(k, min(k + 2, 9 * kd + 9)) for k in range(9 * kd, 9 * kd + 9, 2)]


def local_share_kernel(order, volume, cot_in_hbm, turned, share, wide, taps, cot, sems):
    (copy,) = start_all([(cot_in_hbm, cot)], sems)
    for i in range(SLAB):
        fill_taps(volume.at[i], i, wide, taps)
    copy.wait()
    for j in range(SLAB * CELLS // 256):
        rows = pl.ds(j * 256, 256)
        turned[:, rows] = lax.dot_general(
            order[...], cot[rows, :], (((1,), (1,)), ((), ())), preferred_element_type=f32
        ).astype(bf16)
    for kd in range(3):
        for some in tap_groups(kd):
            total = None
            for d in range(SLAB):
                if 0 <= d + kd - 1 < SLAB:
                    part = product(turned[:, pl.ds(d * CELLS, CELLS)], taps_at(taps, d + kd - 1, some))
                    total = part if total is None else total + part
            share[:, pl.ds(some[0] * CIN, len(some) * CIN)] = total


def local_share(*args):
    outs = (shaped(bf16, COUT, SLAB * CELLS), shaped(f32, COUT, COLUMNS))
    own_copy = [pltpu.VMEM((SLAB * CELLS, COUT), bf16), pltpu.SemaphoreType.DMA((1,))]
    return call(
        local_share_kernel,
        outs,
        args,
        taps_scratch(2) + own_copy,
        FLOPS * 2 // 3,
        specs=[IN_VMEM, IN_VMEM, IN_HBM],
        name="local_share",
    )


def edge_share_kernel(core, near, far, turned, share, keep, send, wide, taps):
    c = core[0]
    fill_taps(near, 1 - c, wide, taps)
    fill_taps(far, c, wide, taps)
    for kd in range(3):
        for some in tap_groups(kd):
            lanes = pl.ds(some[0] * CIN, len(some) * CIN)
            total = share[:, lanes]
            if kd != 1:
                edge = kd // 2
                total = total + product(turned[:, pl.ds(edge * CELLS, CELLS)], taps_at(taps, edge, some))
            keep[:, lanes] = total[: COUT // 2]
            send[:, lanes] = total[COUT // 2 :].astype(bf16)


def edge_share(core, near, far, turned, share):
    outs = (shaped(f32, COUT // 2, COLUMNS), shaped(bf16, COUT // 2, COLUMNS))
    args = (core, near, far, turned, share)
    return call(edge_share_kernel, outs, args, taps_scratch(2), FLOPS // 3, name="edge_share")


def start_all(pairs, sems):
    copies = [pltpu.make_async_copy(source, target, sems.at[i]) for i, (source, target) in enumerate(pairs)]
    for copy in copies:
        copy.start()
    return copies


def forward_body(core, near, volume, far, weight_in_hbm, out, scratch, between):
    planes, weight, result, sems = scratch[-4:]
    wide, taps = scratch[:4], scratch[4:8]
    first = core[0] == 0
    *own, near_copy, far_copy, whole = start_all(
        [
            (volume.at[0], planes.at[0]),
            (volume.at[1], planes.at[1]),
            (near, planes.at[2]),
            (far, planes.at[3]),
            (weight_in_hbm, weight),
        ],
        sems,
    )
    for i in range(SLAB):
        own[i].wait()
        fill_taps(planes[i], 0, wide[1 + i], taps[1 + i])
    near_copy.wait()
    far_copy.wait()
    fill_taps(jnp.where(first, planes[3], planes[2]), 0, wide[0], taps[0])
    fill_taps(jnp.where(first, planes[2], planes[3]), 0, wide[3], taps[3])
    whole.wait()
    between()
    writes = []
    for d in range(SLAB):
        parts = [taps[d + k // 9][0, pl.ds(k // 3 % 3 * SIDE, CELLS), pl.ds(k % 3 * CIN, CIN)] for k in range(TAPS)]
        pre = product(jnp.concatenate(parts, axis=1), weight[...])
        result[d] = jnp.where(pre >= 0, pre, 0.3 * pre).astype(bf16)
        writes.append(pltpu.make_async_copy(result.at[d], out.at[pl.ds(d * CELLS, CELLS)], sems.at[5 + d]))
        writes[d].start()
    return writes


def forward_scratch():
    wide, taps = taps_scratch(1)
    return [wide] * 4 + [taps] * 4 + [
        pltpu.VMEM((4, CELLS, CIN), bf16),
        pltpu.VMEM((COLUMNS, COUT), bf16),
        pltpu.VMEM((SLAB, CELLS, COUT), bf16),
        pltpu.SemaphoreType.DMA((7,)),
    ]


def sum_rows_kernel(parts, rows, spread):
    total = parts[0].astype(f32)
    for i in range(1, parts.shape[0]):
        total = total + parts[i].astype(f32)
    for k in range(TAPS):
        spread[:, k, :] = total[:, k * CIN : (k + 1) * CIN]
    rows[...] = spread[...].astype(bf16)


def sum_rows(parts):
    shape = (parts.shape[1], TAPS, CIN)
    return call(sum_rows_kernel, (shaped(bf16, *shape),), (parts,), [pltpu.VMEM(shape, f32)], name="sum_rows")[0]


def finish(parts, count):
    def kernel(parts, row):
        total = jnp.sum(parts[...].astype(f32), axis=0) / jnp.sqrt(f32(count))
        for k in range(TAPS):
            row[:, pl.ds(k * CIN, CIN)] = total[k : k + 1, :]

    return call(kernel, (shaped(f32, 1, COLUMNS),), (parts,), name="finish")[0]


def turn_weight_kernel(weight, turned):
    for k in range(TAPS):
        turned[pl.ds(k // 3 * COUT, COUT), pl.ds(k % 3 * CIN, CIN)] = weight[pl.ds(k * CIN, CIN), :].T


def turn_weight(weight):
    return call(turn_weight_kernel, (shaped(bf16, 9 * COUT, 3 * CIN),), (weight,), name="turn_weight")[0]


def input_grad_copies(d, halo, cot, turned, scratch, whole):
    padded, weight, _, _, sems = scratch
    middle = pl.ds(SIDE, CELLS)
    mine = pl.ds(pl.multiple_of(d * CELLS, CELLS), CELLS)
    other = pl.ds(pl.multiple_of((1 - d) * CELLS, CELLS), CELLS)
    planes = [cot.at[mine], cot.at[other], halo.at[other] if whole else halo]
    pairs = []
    for slot, kd in enumerate((1, 2 * d, 2 - 2 * d)):
        rows = pl.ds(pl.multiple_of(kd * 3 * COUT, 3 * COUT), 3 * COUT)
        pairs += [(planes[slot], padded.at[slot, middle]), (turned.at[rows], weight.at[slot])]
    return start_all(pairs, sems)


def input_grad_body(d, copies, out, scratch):
    padded, weight, sums, result, sems = scratch
    zero = jnp.zeros((SIDE, COUT), bf16)
    inner = pl.ds(8, CELLS)
    for slot in range(3):
        padded[slot, pl.ds(0, SIDE), :] = zero
        padded[slot, pl.ds(SIDE + CELLS, SIDE), :] = zero
        for copy in copies[2 * slot : 2 * slot + 2]:
            copy.wait()
        parts = [padded[slot, pl.ds((2 - kh) * SIDE, CELLS), :] for kh in range(3)]
        part = product(jnp.concatenate(parts, axis=1), weight[slot])
        sums[inner, :] = part if slot == 0 else sums[inner, :] + part
    col = lax.broadcasted_iota(jnp.int32, (CELLS, CIN), 0) % SIDE
    total = sums[inner, pl.ds(CIN, CIN)]
    total = total + jnp.where(col < SIDE - 1, sums[pl.ds(9, CELLS), pl.ds(0, CIN)], 0.0)
    total = total + jnp.where(col > 0, sums[pl.ds(7, CELLS), pl.ds(2 * CIN, CIN)], 0.0)
    result[...] = total.astype(bf16)
    write = pltpu.make_async_copy(result, out.at[pl.ds(pl.multiple_of(d * CELLS, CELLS), CELLS)], sems.at[6])
    write.start()
    return write


INPUT_GRAD_SCRATCH = [
    pltpu.VMEM((3, PADDED, COUT), bf16),
    pltpu.VMEM((3, 3 * COUT, 3 * CIN), bf16),
    pltpu.VMEM((CELLS + 16, 3 * CIN), f32),
    pltpu.VMEM((CELLS, CIN), bf16),
    pltpu.SemaphoreType.DMA((7,)),
]


def near_kernel(core, near, volume, far, weight, halo, cot, turned, out, grad, *scratch):
    d = 1 - core[0]
    mine, other = scratch[:12], scratch[12:]
    copies = []

    def between():
        copies.extend(input_grad_copies(d, halo, cot, turned, other, True))

    writes = forward_body(core, near, volume, far, weight, out, mine, between)
    writes.append(input_grad_body(d, copies, grad, other))
    for write in writes:
        write.wait()


def forward_and_near(*args):
    return call(
        near_kernel,
        (shaped(bf16, SLAB * CELLS, COUT), shaped(bf16, SLAB * CELLS, CIN)),
        args,
        forward_scratch() + INPUT_GRAD_SCRATCH,
        FLOPS * 3 // 2,
        specs=[IN_SMEM] + [IN_HBM] * (len(args) - 1),
        out_specs=(IN_HBM, IN_HBM),
        vmem=VMEM_MORE,
        name="forward_and_near",
    )


def far_kernel(core, halo, cot, turned, earlier, grad, *scratch):
    d = core[0]
    copies = input_grad_copies(d, halo, cot, turned, scratch, False)
    input_grad_body(d, copies, grad, scratch).wait()


def far_plane(*args):
    return call(
        far_kernel,
        (shaped(bf16, SLAB * CELLS, CIN),),
        args,
        INPUT_GRAD_SCRATCH,
        FLOPS // 2,
        specs=[IN_SMEM] + [IN_HBM] * (len(args) - 1),
        out_specs=(IN_HBM,),
        input_output_aliases={4: 0},
        vmem=VMEM_MORE,
        name="input_grad_far",
    )[0]


def from_core(value):
    return lax.ppermute(value, "space", [(i, i ^ 1) for i in range(16)])


def from_chip(value):
    return lax.ppermute(value, "space", [(i, ((i + 1) ^ 1) - 1) for i in range(1, 15)])


def row_order_kernel(core, order):
    place = lax.broadcasted_iota(jnp.int32, (COUT, COUT), 0)
    row = (place & 127) * 2 + (core[0] ^ (place >> 7))
    order[...] = jnp.where(row == lax.broadcasted_iota(jnp.int32, (COUT, COUT), 1), 1.0, 0.0).astype(bf16)


def row_order(core):
    return call(row_order_kernel, (shaped(bf16, COUT, COUT),), (core,), flops=FLOPS, name="row_order")[0]


def together(*arrays):
    return lax.optimization_barrier(arrays)


def shards(volume, weight, cotangent):
    volume = volume.reshape(SLAB, CELLS, CIN)
    cot = cotangent.reshape(SLAB * CELLS, COUT)
    weight = weight.reshape(COLUMNS, COUT)
    core = lax.axis_index("space").astype(jnp.int32) % 2
    flag = core.reshape(1)

    def plane(i):
        return lax.dynamic_index_in_dim(volume, i, 0, False)

    far, near, order = together(plane(core), plane(1 - core), row_order(flag))
    far, near = from_chip(far), from_core(near)
    turned, share = local_share(order, volume, cot)
    far, near, turned, share = together(far, near, turned, share)
    keep, send = edge_share(flag, near, far, turned, share)

    received = from_core(send)
    weight, send = together(weight, send)
    back_weight = turn_weight(weight)
    whole, back_weight = together(cot, back_weight)
    cot_far, cot_near = from_chip(lax.dynamic_slice_in_dim(whole, core * CELLS, CELLS)), from_core(whole)
    received, back_weight = together(received, back_weight)
    total = keep + received.astype(f32)

    dp = lax.axis_size("dp")
    send = total.astype(bf16).reshape(dp, -1, COLUMNS)
    parts = lax.all_to_all(send, "dp", 0, 0)
    weight, send = together(weight, send)
    activation, input_grad = forward_and_near(flag, near, volume, far, weight, cot_near, cot, back_weight)
    parts, input_grad = together(parts, input_grad)
    send = sum_rows(parts)

    parts = lax.all_to_all(send, "space", 0, 0, axis_index_groups=[list(range(c, 16, 2)) for c in range(2)])
    back_weight, send = together(back_weight, send)
    input_grad = far_plane(flag, cot_far, cot, back_weight, input_grad)
    parts, input_grad = together(parts, input_grad)
    count = dp * lax.axis_size("space") * SLAB * CELLS
    return (
        activation.reshape(1, SLAB, SIDE, SIDE, COUT),
        input_grad.reshape(1, SLAB, SIDE, SIDE, CIN),
        finish(parts, count),
    )


def solution(mesh):
    slabs = P("dp", "space", None, None, None)
    return jax.shard_map(
        shards,
        mesh=mesh,
        in_specs=(slabs, P(), slabs),
        out_specs=(slabs, slabs, P(("dp", "space"), None)),
        check_vma=False,
    )
```
